128 devices in a mesh: rep: 16 (over y, x_hi, core), fsdp: 8 (over x_lo, z).
Axes of the slice: x: 4 (x_hi: 2, x_lo: 2; x = x_hi * 2 + x_lo), y: 4, z: 4, core: 2. Of those that a mesh axis runs over, the one named last changes fastest.
Arguments:
- momentum: float32 [16, 2560, 2560], P('rep', 'fsdp'), may hold values from -6 to 6
- gradient: bfloat16 [16, 2560, 2560], P('rep', 'fsdp'), may hold values from -6 to 6
- weights: bfloat16 [2560, 2560], P('fsdp'), may hold values from -0.125 to 0.125
- inputs: bfloat16 [16, 5120, 2560], P('rep', 'fsdp'), may hold values from -6 to 6
Outputs:
- new_momentum: float32 [16, 2560, 2560], P('rep', 'fsdp')
- update: float32 [2560, 2560], P('fsdp')
- outputs: bfloat16 [16, 5120, 2560], P('rep', 'fsdp')
The draws below stay inside these ranges and needn't reach their ends.
All inputs are finite; a program needn't handle non-finite values.
Results may differ from the reference program's by a relative error of at most 0.005.
Values may be sent and summed in bfloat16 or wider, within the bound.
No kernel may reach another device: no remote copies, remote signals or barrier semaphores. Data moves between devices by JAX's collectives and lax.ppermute only.
A program may use at most 192 MiB of HBM per device.

```python
import math
import jax
import jax.numpy as jnp
from jax import lax

DIN = 2560
DOUT = 2560
TOK_REP = 5120
N_REP = 16


def level_of(own_key, extent, cuts, smallest, high):
    def one(dim, shards_of):
        heights = jax.random.uniform(jax.random.fold_in(jax.random.fold_in(own_key, 6), dim), (shards_of,), jnp.float32, smallest / len(cuts), high / len(cuts))
        return jnp.repeat(jnp.exp(heights), extent[dim] // shards_of).reshape((-1,) + (1,) * (len(extent) - dim - 1))

    gain = one(*cuts[0])
    for cut in cuts[1:]:
        gain = gain * one(*cut)
    return gain


def centred(own_key, dims, scale, limit, cuts=(), held_as=jnp.bfloat16):
    entries = scale * jax.random.normal(own_key, dims, jnp.float32)
    if cuts:
        entries = entries * level_of(own_key, dims, cuts, -0.22, 0.18)
    return jnp.clip(entries, -limit, limit).astype(held_as)


def setup_inputs(seed: int = 0) -> dict:
    keys = jax.random.split(jax.random.key(seed), 5)
    return {
        "momentum": centred(keys[0], (N_REP, DIN, DOUT), 1.0, 6.0, ((0, 16), (1, 8)), jnp.float32),
        "gradient": centred(keys[1], (N_REP, DIN, DOUT), 1.0, 6.0, ((0, 16), (1, 8))),
        "weights": centred(keys[2], (DIN, DOUT), DIN ** -0.5, 0.125, ((0, 8),)),
        "inputs": centred(keys[3], (N_REP, TOK_REP, DIN), 1.0, 6.0, ((0, 16), (1, 8))),
    }


decay = 0.9
step_size = 0.1
highest = lax.Precision.HIGHEST

def dct_basis():
    freq = jnp.arange(16).astype(jnp.float32)[:, None]
    place = jnp.arange(64).astype(jnp.float32)[None, :]
    table = jnp.cos(math.pi * (2.0 * place + 1.0) * freq / 128.0) * math.sqrt(2.0 / 64.0)
    scale = jnp.where(jnp.arange(16)[:, None] == 0, math.sqrt(0.5), 1.0).astype(jnp.float32)
    return (table * scale).astype(jnp.float32)

def column_table(basis, col_count):
    blocks = col_count // 64
    repeated = jnp.tile(basis.T, (blocks, blocks))
    owner_col = jnp.arange(col_count) // 64
    owner_band = jnp.arange(blocks * 16) // 16
    same_block = owner_col[:, None] == owner_band[None, :]
    return jnp.where(same_block, repeated, jnp.zeros_like(repeated)).astype(jnp.float32)

def band_of(field, basis, columns):
    row_count = field.shape[0]
    right_side = jnp.dot(field, columns, precision=highest, preferred_element_type=jnp.float32)
    right_side = right_side.reshape(row_count // 64, 64, right_side.shape[1])
    return jnp.einsum('in,anw->aiw', basis, right_side, precision=highest)

def left_inverse(band, basis):
    blocks = jnp.einsum('in,aiw->anw', basis, band, precision=highest)
    return blocks.reshape(band.shape[0] * 64, band.shape[2])

def right_inverse(partial_value, columns):
    return jnp.dot(partial_value, columns.T, precision=highest, preferred_element_type=jnp.float32)

def reference(momentum, gradient, weights, inputs):
    basis = dct_basis()
    columns = column_table(basis, momentum.shape[2])

    def replica_step(inputs_pair):
        moment = decay * inputs_pair[0] + inputs_pair[1].astype(jnp.float32)
        coeffs = band_of(moment, basis, columns)
        return (moment - right_inverse(left_inverse(coeffs, basis), columns), coeffs)
    new_momentum, coeffs = lax.map(replica_step, (momentum, gradient))
    mean_band = lax.optimization_barrier(jnp.sum(coeffs, axis=0)) / N_REP
    update = right_inverse(left_inverse(mean_band, basis), columns)
    new_weights = (weights.astype(jnp.float32) - step_size * update).astype(jnp.bfloat16)

    def forward(tokens):
        return jnp.dot(tokens, new_weights, preferred_element_type=jnp.float32).astype(jnp.bfloat16)
    outputs = lax.map(forward, inputs)
    return (new_momentum, update, outputs)
```

```python
import functools
import math

import jax
import jax.numpy as jnp
import ml_dtypes
import numpy as np
from jax import lax
from jax.experimental import pallas as pl
from jax.experimental.pallas import tpu as pltpu
from jax.sharding import PartitionSpec as P

f32, bf16 = jnp.float32, jnp.bfloat16
BOTH = ("rep", "fsdp")
decay = 0.9
step_size = 0.1
ROWS, COLS, TOKENS = 320, 2560, 640
BANDS = 16 * COLS // 64
TILE_ROWS = 16 * ROWS // 64
HALF = BANDS // 2
WIDE = 512
NARROW = 128
N_REP = 16


def place_of(device):
    rep, shard = divmod(device, 8)
    return (rep // 2 % 2) * 2 + shard // 4, rep // 4, shard % 4, rep % 2


def device_at(x, y, z, core):
    x, y, z = x % 4, y % 4, z % 4
    return ((y * 2 + x // 2) * 2 + core % 2) * 8 + (x % 2) * 4 + z


def moved(value, first, second=None):
    pairs = []
    for device in range(128):
        x, y, z, core = place_of(device)
        dx, dy, dz, dc = first if second is None or core == 0 else second
        pairs.append((device, device_at(x + dx, y + dy, z + dz, core + dc)))
    return lax.ppermute(value, BOTH, pairs)


def along_z(value):
    return moved(value, (0, 0, 1, 0), (0, 0, -1, 0))


def along_x(value):
    return moved(value, (1, 0, 0, 0), (-1, 0, 0, 0))


def across(value):
    return moved(value, (0, 0, 0, 1))


def by(value, axis, distance):
    return moved(value, tuple(distance if k == axis else 0 for k in range(4)))


def basis_table():
    freq = np.arange(16)[:, None]
    spot = np.arange(64)[None, :]
    table = np.cos(math.pi * (2 * spot + 1) * freq / 128) * math.sqrt(2 / 64)
    table[0] = math.sqrt(1 / 64)
    return table


def halves(table):
    high = table.astype(ml_dtypes.bfloat16)
    low = (table - high.astype(np.float64)).astype(ml_dtypes.bfloat16)
    return high, low


def tables():
    basis = basis_table()
    left_high, left_low = halves(np.kron(np.eye(ROWS // 64), basis))
    right_high, right_low = halves(np.kron(np.eye(WIDE // 64), basis.T))
    step_high, step_low = halves(np.kron(np.eye(4), basis) * (-step_size / N_REP))
    return {
        "left": np.concatenate([left_high, left_low], 0),
        "right": np.stack([right_high, right_low]),
        "left_t": np.concatenate([left_high.T, left_high.T, left_low.T], 1),
        "right_t": np.concatenate([right_high.T, right_high.T, right_low.T], 0),
        "right_pair": np.concatenate([right_high, right_low], 1),
        "step": np.concatenate([step_high, step_high, step_low, step_low], 0),
    }


def dot(a, b):
    return jnp.dot(a, b, preferred_element_type=f32)


def split(value):
    high = value.astype(bf16)
    return high, (value - high.astype(f32)).astype(bf16)


def core_of():
    return lax.rem(lax.axis_index("rep"), 2)


def whole(shape):
    return pl.BlockSpec(shape, lambda j: (0,) * len(shape))


ANY = pl.BlockSpec(memory_space=pl.ANY)
VMEM = pl.BlockSpec(memory_space=pltpu.VMEM)


def params(megabytes):
    return pltpu.CompilerParams(vmem_limit_bytes=megabytes * 2**20)


def call(kernel, ins, outs, scratch=(), grid=(), megabytes=24, name=None, after=(), through=()):
    n_in, n_out, n_extra = len(ins), len(outs), len(after) + len(through)
    token = ((8, 128), f32, whole((8, 128)) if grid else VMEM)

    def body(*refs):
        n = n_in + n_extra
        token_ref = refs[n + n_out]
        token_ref[...] = jnp.zeros(token_ref.shape, f32)
        kernel(*refs[:n_in], *refs[n : n + n_out], *refs[n + n_out + 1 + len(through) :])

    return pl.pallas_call(
        body,
        grid=grid,
        out_shape=tuple(jax.ShapeDtypeStruct(shape, dtype) for shape, dtype, _ in (*outs, token))
        + tuple(jax.ShapeDtypeStruct(array.shape, array.dtype) for array in through),
        in_specs=[spec for _, spec in ins] + [ANY] * n_extra,
        out_specs=tuple(spec for _, _, spec in (*outs, token)) + (ANY,) * len(through),
        scratch_shapes=list(scratch),
        input_output_aliases={
            n_in + len(after) + k: n_out + 1 + k for k in range(len(through))
        },
        compiler_params=params(megabytes),
        cost_estimate=pl.CostEstimate(flops=1, transcendentals=0, bytes_accessed=1),
        name=name,
    )(*[array for array, _ in ins], *after, *through)


def column_block(rows, width):
    return pl.BlockSpec((rows, width), lambda j: (0, j))


def column_block_of_one(rows, width):
    return pl.BlockSpec((1, rows, width), lambda j: (0, 0, j))


N_WIDE = COLS // WIDE
HALF_ROWS = ROWS // 2
QUARTER = ROWS // 4


def band_kernel(
    m_ref, g_ref, w_ref, left_ref, right_ref,
    c_ref, mine_ref, theirs_ref, moment_ref, first_ref, second_ref,
    g_buffer, left, right, sems,
):
    core = core_of()

    def copies(j):
        columns = pl.ds(j * WIDE, WIDE)
        return (
            pltpu.make_async_copy(m_ref.at[0, :, columns], moment_ref.at[:, columns], sems.at[2 * j]),
            pltpu.make_async_copy(g_ref.at[0, :, columns], g_buffer.at[:, columns], sems.at[2 * j + 1]),
        )

    def rows(which):
        return w_ref.at[pl.ds(pl.multiple_of(which * HALF_ROWS, HALF_ROWS), HALF_ROWS)]

    base = 2 * N_WIDE
    others = (
        pltpu.make_async_copy(left_ref, left, sems.at[base]),
        pltpu.make_async_copy(right_ref, right, sems.at[base + 1]),
        pltpu.make_async_copy(rows(core), first_ref, sems.at[base + 2]),
        pltpu.make_async_copy(rows(1 - core), second_ref, sems.at[base + 3]),
    )
    for copy in (*others[:2], *copies(0), *copies(1), *copies(2), *copies(3), *copies(4), *others[2:]):
        copy.start()
    for copy in others[:2]:
        copy.wait()
    for j in range(N_WIDE):
        for copy in copies(j):
            copy.wait()
        columns = slice(j * WIDE, (j + 1) * WIDE)
        moment = decay * moment_ref[:, columns] + g_buffer[:, columns].astype(f32)
        moment_ref[:, columns] = moment
        high, low = split(moment)
        both = dot(left[...], high)
        value = both[:TILE_ROWS] + both[TILE_ROWS:] + dot(left[:TILE_ROWS], low)
        high, low = split(value)
        c_ref[:, j * NARROW : (j + 1) * NARROW] = (
            dot(high, right[0]) + dot(high, right[1]) + dot(low, right[0])
        )
    is_first = core == 0
    one, two = c_ref[:, :HALF], c_ref[:, HALF:]
    mine_ref[...] = jnp.where(is_first, one, two)
    theirs_ref[...] = jnp.where(is_first, two, one)
    for copy in others[2:]:
        copy.wait()


def band(momentum, gradient, weights, table, **order):
    part = ((TILE_ROWS, HALF), f32, VMEM)
    rows = ((HALF_ROWS, COLS), bf16, VMEM)
    return call(
        band_kernel,
        [(array, ANY) for array in (momentum, gradient, weights, table["left"], table["right"])],
        [((TILE_ROWS, BANDS), f32, VMEM), part, part, ((ROWS, COLS), f32, VMEM), rows, rows],
        scratch=[
            pltpu.VMEM((ROWS, COLS), bf16),
            pltpu.VMEM((2 * TILE_ROWS, ROWS), bf16),
            pltpu.VMEM((2, WIDE, NARROW), bf16),
            pltpu.SemaphoreType.DMA((2 * N_WIDE + 4,)),
        ],
        name="band",
        **order,
    )


def field_of(band, left_t, right_t):
    high, low = split(band)
    value = dot(jnp.concatenate([high, low, high], axis=1), right_t)
    high, low = split(value)
    return dot(left_t, jnp.concatenate([high, low, high], axis=0))


def momentum_kernel(moment_ref, c_ref, left_ref, right_ref, out_ref):
    columns = pl.ds(pl.multiple_of(pl.program_id(0) * WIDE, WIDE), WIDE)
    bands = pl.ds(pl.multiple_of(pl.program_id(0) * NARROW, NARROW), NARROW)
    out_ref[0] = moment_ref[:, columns] - field_of(
        c_ref[:, bands], left_ref[...], right_ref[...]
    )


def momentum_less_band(moment, coeffs, table, **order):
    return call(
        momentum_kernel,
        [
            (moment, VMEM),
            (coeffs, VMEM),
            (table["left_t"], VMEM),
            (table["right_t"], VMEM),
        ],
        [((1, ROWS, COLS), f32, column_block_of_one(ROWS, WIDE))],
        grid=(COLS // WIDE,),
        name="momentum_less_band",
        **order,
    )


def update_kernel(mine_ref, theirs_ref, left_ref, right_ref, out_ref, total):
    j = pl.program_id(0)

    @pl.when(j == 0)
    def _():
        is_first = core_of() == 0
        mine, theirs = mine_ref[...] / N_REP, theirs_ref[...] / N_REP
        first = jnp.where(is_first, mine, theirs)
        second = jnp.where(is_first, theirs, mine)
        full = jnp.concatenate([first, second], axis=1)
        for k in range(5):
            total[k] = full[:, k * NARROW : (k + 1) * NARROW]

    out_ref[...] = field_of(total[j], left_ref[...], right_ref[...])


def update_of(mine, theirs, table, **order):
    return call(
        update_kernel,
        [
            (mine, whole((TILE_ROWS, HALF))),
            (theirs, whole((TILE_ROWS, HALF))),
            (table["left_t"], whole((ROWS, 3 * TILE_ROWS))),
            (table["right_t"], whole((3 * NARROW, WIDE))),
        ],
        [((ROWS, COLS), f32, column_block(ROWS, WIDE))],
        scratch=[pltpu.VMEM((5, TILE_ROWS, NARROW), f32)],
        grid=(COLS // WIDE,),
        name="update",
        **order,
    )


SIDES = (3, 0, 1, 2)


def input_band_kernel(x_ref, pair_ref, high_ref, low_ref, turned_ref, held, pair, sems):
    def copy(j):
        columns = pl.ds(j * WIDE, WIDE)
        return pltpu.make_async_copy(x_ref.at[0, :, columns], held.at[:, columns], sems.at[j])

    table = pltpu.make_async_copy(pair_ref, pair, sems.at[N_WIDE])
    table.start()
    for j in range(N_WIDE):
        copy(j).start()
    table.wait()
    for j in range(N_WIDE):
        copy(j).wait()
        both = dot(held[:, j * WIDE : (j + 1) * WIDE], pair[...])
        bands = slice(j * NARROW, (j + 1) * NARROW)
        high_ref[:, bands], low_ref[:, bands] = split(both[:, :NARROW] + both[:, NARROW:])
    shard = lax.axis_index("fsdp")
    here, z = shard // 4, lax.rem(shard, 4)
    wide = COLS // 2
    for k in range(4):

        @pl.when(z == k)
        def _():
            for part, x in enumerate((here, 1 - here)):
                source = held[:, pl.ds(pl.multiple_of(x * wide, NARROW), wide)]
                starts = [(k + side) % 4 * ROWS for side in SIDES]
                turned_ref[:, part * wide : (part + 1) * wide] = jnp.concatenate(
                    [source[:, start : start + ROWS] for start in starts], axis=1
                )


def input_band(inputs, table, **order):
    part = ((TOKENS, BANDS), bf16, VMEM)
    return call(
        input_band_kernel,
        [(inputs, ANY), (table["right_pair"], ANY)],
        [part, part, ((TOKENS, COLS), bf16, VMEM)],
        scratch=[
            pltpu.VMEM((TOKENS, COLS), bf16),
            pltpu.VMEM((WIDE, 2 * NARROW), bf16),
            pltpu.SemaphoreType.DMA((N_WIDE + 1,)),
        ],
        name="input_band",
        **order,
    )


def sum_kernel(*refs):
    total = refs[0][...]
    for ref in refs[1:-1]:
        total += ref[...]
    refs[-1][...] = total


def sum_of(parts, name, **order):
    return call(
        sum_kernel,
        [(part, VMEM) for part in parts],
        [(parts[0].shape, f32, VMEM)],
        name=name,
        **order,
    )


def both_kernel(own_ref, other_ref, out_ref):
    is_first = lax.axis_index("fsdp") < 4
    own, other = own_ref[...], other_ref[...]
    out_ref[:TILE_ROWS] = jnp.where(is_first, own, other)
    out_ref[TILE_ROWS:] = jnp.where(is_first, other, own)


def both_of(own, other, **order):
    return call(
        both_kernel,
        [(own, VMEM), (other, VMEM)],
        [((2 * TILE_ROWS, HALF), f32, VMEM)],
        name="both",
        **order,
    )


def pair_kernel(one_ref, two_ref, own_ref, pair_ref):
    total = one_ref[...] + two_ref[...]
    is_first = lax.axis_index("fsdp") < 4
    own_ref[...] = jnp.where(is_first, total[:TILE_ROWS], total[TILE_ROWS:])
    pair_ref[...] = total.astype(bf16)


def pair_of(one, two, **order):
    return call(
        pair_kernel,
        [(one, VMEM), (two, VMEM)],
        [((TILE_ROWS, HALF), f32, VMEM), ((2 * TILE_ROWS, HALF), bf16, VMEM)],
        name="pair",
        **order,
    )


def quad_kernel(pair_ref, other_ref, out_ref):
    is_even = lax.rem(lax.axis_index("fsdp"), 2) == 0
    rows = 2 * TILE_ROWS
    pair, other = pair_ref[...], other_ref[...]
    out_ref[:rows] = jnp.where(is_even, pair, other)
    out_ref[rows:] = jnp.where(is_even, other, pair)


def quad_of(pair, other, **order):
    return call(
        quad_kernel,
        [(pair, VMEM), (other, VMEM)],
        [((4 * TILE_ROWS, HALF), bf16, VMEM)],
        name="quad",
        **order,
    )


def hand_on_kernel():
    pass


def hand_on(arrays, after, name):
    return call(hand_on_kernel, [], [], name=name, after=after, through=arrays)[1:]


def change_kernel(high_ref, low_ref, here_ref, there_ref, s_here_ref, s_there_ref, out_ref):
    is_first = core_of() == 0
    is_low = lax.rem(lax.axis_index("fsdp"), 4) < 2
    here = here_ref[...], s_here_ref[...]
    there = there_ref[...], s_there_ref[...]
    for half in range(2):
        near = jnp.where(is_first, here[half], here[1 - half])
        far = jnp.where(is_first, there[half], there[1 - half])
        one, two = jnp.where(is_low, near, far), jnp.where(is_low, far, near)
        blocks = [part[k * TILE_ROWS : (k + 1) * TILE_ROWS] for part in (one, two) for k in range(4)]
        total = jnp.concatenate([blocks[2 * z + x] for x in range(2) for z in range(4)], axis=0)
        value = dot(high_ref[...], total) + dot(low_ref[...], total)
        for k in range(5):
            high, low = split(value[:, k * 64 : (k + 1) * 64])
            start = (half * 5 + k) * 256
            out_ref[:, start : start + 256] = jnp.concatenate([high, low, high, low], axis=1)


def change_of(high, low, quads, **order):
    return call(
        change_kernel,
        [(array, VMEM) for array in (high, low, *quads)],
        [((TOKENS, COLS), bf16, VMEM)],
        name="change",
        **order,
    )


BLOCK = 512
N_BLOCKS = COLS // BLOCK


def beside(core, first, s_first, second, s_second, columns):
    is_first = core == 0
    a, sa, b, sb = (ref[:, columns] for ref in (first, s_first, second, s_second))
    before = [jnp.where(is_first, a, sa), jnp.where(is_first, b, sb)]
    behind = [jnp.where(is_first, sb, b), jnp.where(is_first, sa, a)]
    return before, behind


def in_order(core, one, other, columns):
    is_first = core == 0
    a, b = one[:, columns], other[:, columns]
    return [jnp.where(is_first, a, b), jnp.where(is_first, b, a)]


def own_kernel(x_ref, w_ref, z0, sz0, z1, sz1, z2, sz2, out_ref):
    core = core_of()
    for n in range(N_BLOCKS):
        columns = slice(n * BLOCK, (n + 1) * BLOCK)
        before, behind = beside(core, z0, sz0, z1, sz1, columns)
        rows = before + [w_ref[:, columns]] + behind + in_order(core, z2, sz2, columns)
        out_ref[:, columns] = dot(x_ref[:, : 4 * ROWS], jnp.concatenate(rows, axis=0))


def own_product(turned, pieces, **order):
    return call(
        own_kernel,
        [(array, VMEM) for array in (turned, *pieces)],
        [((TOKENS, COLS), f32, VMEM)],
        name="own_product",
        **order,
    )


def rest_kernel(
    x_ref, acc_ref, change_ref, step_ref,
    x0, sx0, z0, sz0, z1, sz1, top, s_top, low, s_low, out_ref,
):
    core = core_of()
    columns = pl.ds(pl.multiple_of(pl.program_id(0) * BLOCK, BLOCK), BLOCK)
    before, behind = beside(core, z0, sz0, z1, sz1, columns)
    tops, lows = in_order(core, top, s_top, columns), in_order(core, low, s_low, columns)
    rows = before + in_order(core, x0, sx0, columns) + behind
    rows += [tops[0], lows[0], tops[1], lows[1]]
    change = change_ref[:, columns]
    steps = [dot(change[:, k : k + 256], step_ref[...]) for k in (0, 256)]
    value = dot(x_ref[:, 4 * ROWS :], jnp.concatenate(rows, axis=0))
    out_ref[0] = (acc_ref[:, columns] + value + jnp.concatenate(steps, axis=1)).astype(bf16)


def rest_product(turned, acc, change, pieces, table, **order):
    return call(
        rest_kernel,
        [(array, VMEM) for array in (turned, acc, change, table["step"], *pieces)],
        [((1, TOKENS, COLS), bf16, column_block_of_one(TOKENS, BLOCK))],
        grid=(N_BLOCKS,),
        name="rest_product",
        **order,
    )


def swapped(value, axis, step):
    pairs = []
    for device in range(128):
        place = list(place_of(device))
        place[axis] = 3 - place[axis] if step else place[axis] ^ 1
        pairs.append((device, device_at(*place)))
    return lax.ppermute(value, BOTH, pairs)


def shards(momentum, gradient, weights, inputs):
    table = {
        name: pltpu.with_memory_space_constraint(jnp.asarray(value), pltpu.HBM)
        if name in ("left", "right", "right_pair")
        else value
        for name, value in tables().items()
    }
    momentum, gradient, weights, inputs = (
        pltpu.with_memory_space_constraint(array, pltpu.HBM)
        for array in (momentum, gradient, weights, inputs)
    )

    coeffs, mine, theirs, moment, first, second, _ = band(momentum, gradient, weights, table)
    z0 = along_z(first)
    x0 = along_x(first)
    z1 = along_z(second)
    chip, _ = sum_of([mine, across(theirs)], "chip_sum")
    half_y = swapped(chip, 1, 0)
    high, low, turned, done = input_band(inputs, table, after=[chip])
    half_sum, _, z0, x0 = sum_of(
        [chip, half_y], "half_y_sum", after=[done], through=[z0, x0]
    )
    rest_y = swapped(half_sum, 1, 1)
    xz0 = along_x(z0)
    z2 = along_z(z0)
    sz0 = across(z0)
    column, _, z1, sz0, x0 = sum_of([half_sum, rest_y], "y_sum", through=[z1, sz0, x0])
    half_x = swapped(column, 0, 0)
    xz1 = along_x(z1)
    sz1 = across(z1)
    both, _, xz0, z2, x0, sz1 = both_of(column, half_x, through=[xz0, z2, x0, sz1])
    rest_x = swapped(both, 0, 1)
    sx0, sz2, sxz0 = across(x0), across(z2), across(xz0)
    new_momentum, done = momentum_less_band(moment, coeffs, table, after=[both])
    own, pair, _, xz1, sx0, sz2, sxz0, z2, xz0 = pair_of(
        both, rest_x, after=[done], through=[xz1, sx0, sz2, sxz0, z2, xz0]
    )
    half_z = swapped(pair, 2, 0)
    s_own, sxz1 = across(own), across(xz1)
    xz2 = along_x(z2[:QUARTER])
    z3 = along_z(xz0[QUARTER:])
    update, done = update_of(own, s_own, table, after=[pair])
    quad, _, sxz1 = quad_of(pair, half_z, after=[done], through=[sxz1])
    rest_z = swapped(quad, 2, 1)
    s_quad = across(quad)
    acc, done, s_quad = own_product(
        turned, [weights, z0, sz0, z1, sz1, z2, sz2], after=[quad], through=[s_quad]
    )
    rest_z, xz2, z3 = hand_on([rest_z, xz2, z3], [done], "after_own_product")
    change, _ = change_of(high, low, [quad, rest_z, s_quad, across(rest_z)])
    result, _ = rest_product(
        turned,
        acc,
        change,
        [x0, sx0, xz0, sxz0, xz1, sxz1, xz2, across(xz2), z3, across(z3)],
        table,
    )
    return (new_momentum, update, result)


def solution(mesh):
    placed = (
        P("rep", "fsdp", None),
        P("rep", "fsdp", None),
        P("fsdp", None),
        P("rep", "fsdp", None),
    )
    return jax.shard_map(
        shards,
        mesh=mesh,
        in_specs=placed,
        out_specs=(P("rep", "fsdp", None), P("fsdp", None), P("rep", "fsdp", None)),
        check_vma=False,
    )
```

```python
import functools
import math

import jax
import jax.numpy as jnp
import ml_dtypes
import numpy as np
from jax import lax
from jax.experimental import pallas as pl
from jax.experimental.pallas import tpu as pltpu
from jax.sharding import PartitionSpec as P

f32, bf16 = jnp.float32, jnp.bfloat16
BOTH = ("rep", "fsdp")
decay = 0.9
step_size = 0.1
ROWS, COLS, TOKENS = 320, 2560, 640
BANDS = 16 * COLS // 64
TILE_ROWS = 16 * ROWS // 64
HALF = BANDS // 2
WIDE = 512
NARROW = 128
N_REP = 16


def place_of(device):
    rep, shard = divmod(device, 8)
    return (rep // 2 % 2) * 2 + shard // 4, rep // 4, shard % 4, rep % 2


def device_at(x, y, z, core):
    x, y, z = x % 4, y % 4, z % 4
    return ((y * 2 + x // 2) * 2 + core % 2) * 8 + (x % 2) * 4 + z


def moved(value, first, second=None):
    pairs = []
    for device in range(128):
        x, y, z, core = place_of(device)
        dx, dy, dz, dc = first if second is None or core == 0 else second
        pairs.append((device, device_at(x + dx, y + dy, z + dz, core + dc)))
    return lax.ppermute(value, BOTH, pairs)


def along_z(value):
    return moved(value, (0, 0, 1, 0), (0, 0, -1, 0))


def along_x(value):
    return moved(value, (1, 0, 0, 0), (-1, 0, 0, 0))


def across(value):
    return moved(value, (0, 0, 0, 1))


def by(value, axis, distance):
    return moved(value, tuple(distance if k == axis else 0 for k in range(4)))


def basis_table():
    freq = np.arange(16)[:, None]
    spot = np.arange(64)[None, :]
    table = np.cos(math.pi * (2 * spot + 1) * freq / 128) * math.sqrt(2 / 64)
    table[0] = math.sqrt(1 / 64)
    return table


def halves(table):
    high = table.astype(ml_dtypes.bfloat16)
    low = (table - high.astype(np.float64)).astype(ml_dtypes.bfloat16)
    return high, low


def tables():
    basis = basis_table()
    left_high, left_low = halves(np.kron(np.eye(ROWS // 64), basis))
    right_high, right_low = halves(np.kron(np.eye(WIDE // 64), basis.T))
    step_high, step_low = halves(np.kron(np.eye(4), basis) * (-step_size / N_REP))
    return {
        "left": np.concatenate([left_high, left_low], 0),
        "right": np.stack([right_high, right_low]),
        "left_t": np.concatenate([left_high.T, left_high.T, left_low.T], 1),
        "right_t": np.concatenate([right_high.T, right_high.T, right_low.T], 0),
        "right_pair": np.concatenate([right_high, right_low], 1),
        "step": np.concatenate([step_high, step_high, step_low, step_low], 0),
    }


def dot(a, b):
    return jnp.dot(a, b, preferred_element_type=f32)


def split(value):
    high = value.astype(bf16)
    return high, (value - high.astype(f32)).astype(bf16)


def core_of():
    return lax.rem(lax.axis_index("rep"), 2)


def whole(shape):
    return pl.BlockSpec(shape, lambda j: (0,) * len(shape))


ANY = pl.BlockSpec(memory_space=pl.ANY)
VMEM = pl.BlockSpec(memory_space=pltpu.VMEM)


def params(megabytes):
    return pltpu.CompilerParams(vmem_limit_bytes=megabytes * 2**20)


def call(kernel, ins, outs, scratch=(), grid=(), megabytes=24, name=None, after=(), through=(), cost=1, held=()):
    n_in, n_out, n_extra = len(ins), len(outs), len(after) + len(through)
    token = ((8, 128), f32, whole((8, 128)) if grid else VMEM)

    def body(*refs):
        n = n_in + n_extra
        token_ref = refs[n + n_out]
        token_ref[...] = jnp.zeros(token_ref.shape, f32)
        kernel(*refs[:n_in], *refs[n : n + n_out], *refs[n + n_out + 1 + len(through) :])

    return pl.pallas_call(
        body,
        grid=grid,
        out_shape=tuple(
            pltpu.VMEM(shape, dtype) if spec is VMEM and shape in held else jax.ShapeDtypeStruct(shape, dtype)
            for shape, dtype, spec in (*outs, token)
        )
        + tuple(jax.ShapeDtypeStruct(array.shape, array.dtype) for array in through),
        in_specs=[spec for _, spec in ins] + [ANY] * n_extra,
        out_specs=tuple(spec for _, _, spec in (*outs, token)) + (ANY,) * len(through),
        scratch_shapes=list(scratch),
        input_output_aliases={
            n_in + len(after) + k: n_out + 1 + k for k in range(len(through))
        },
        compiler_params=params(megabytes),
        cost_estimate=pl.CostEstimate(flops=cost, transcendentals=0, bytes_accessed=1),
        name=name,
    )(*[array for array, _ in ins], *after, *through)


def column_block(rows, width):
    return pl.BlockSpec((rows, width), lambda j: (0, j))


def column_block_of_one(rows, width):
    return pl.BlockSpec((1, rows, width), lambda j: (0, 0, j))


N_WIDE = COLS // WIDE
HALF_ROWS = ROWS // 2
QUARTER = ROWS // 4


def band_kernel(
    m_ref, g_ref, w_ref, left_ref, right_ref,
    c_ref, mine_ref, theirs_ref, moment_ref, first_ref, second_ref,
    g_buffer, left, right, sems,
):
    core = core_of()

    def copies(j):
        columns = pl.ds(j * WIDE, WIDE)
        return (
            pltpu.make_async_copy(m_ref.at[0, :, columns], moment_ref.at[:, columns], sems.at[2 * j]),
            pltpu.make_async_copy(g_ref.at[0, :, columns], g_buffer.at[:, columns], sems.at[2 * j + 1]),
        )

    def rows(which):
        return w_ref.at[pl.ds(pl.multiple_of(which * HALF_ROWS, HALF_ROWS), HALF_ROWS)]

    base = 2 * N_WIDE
    others = (
        pltpu.make_async_copy(left_ref, left, sems.at[base]),
        pltpu.make_async_copy(right_ref, right, sems.at[base + 1]),
        pltpu.make_async_copy(rows(core), first_ref, sems.at[base + 2]),
        pltpu.make_async_copy(rows(1 - core), second_ref, sems.at[base + 3]),
    )
    for copy in (*others[:2], *copies(0), *copies(1), *copies(2), *copies(3), *copies(4), *others[2:]):
        copy.start()
    for copy in others[:2]:
        copy.wait()
    for j in range(N_WIDE):
        for copy in copies(j):
            copy.wait()
        columns = slice(j * WIDE, (j + 1) * WIDE)
        moment = decay * moment_ref[:, columns] + g_buffer[:, columns].astype(f32)
        moment_ref[:, columns] = moment
        high, low = split(moment)
        both = dot(left[...], high)
        value = both[:TILE_ROWS] + both[TILE_ROWS:] + dot(left[:TILE_ROWS], low)
        high, low = split(value)
        c_ref[:, j * NARROW : (j + 1) * NARROW] = (
            dot(high, right[0]) + dot(high, right[1]) + dot(low, right[0])
        )
    is_first = core == 0
    one, two = c_ref[:, :HALF], c_ref[:, HALF:]
    mine_ref[...] = jnp.where(is_first, one, two)
    theirs_ref[...] = jnp.where(is_first, two, one)
    for copy in others[2:]:
        copy.wait()


def band(momentum, gradient, weights, table, **order):
    part = ((TILE_ROWS, HALF), f32, VMEM)
    rows = ((HALF_ROWS, COLS), bf16, VMEM)
    return call(
        band_kernel,
        [(array, ANY) for array in (momentum, gradient, weights, table["left"], table["right"])],
        [((TILE_ROWS, BANDS), f32, VMEM), part, part, ((ROWS, COLS), f32, VMEM), rows, rows],
        scratch=[
            pltpu.VMEM((ROWS, COLS), bf16),
            pltpu.VMEM((2 * TILE_ROWS, ROWS), bf16),
            pltpu.VMEM((2, WIDE, NARROW), bf16),
            pltpu.SemaphoreType.DMA((2 * N_WIDE + 4,)),
        ],
        name="band",
        **order,
    )


def field_of(band, left_t, right_t):
    high, low = split(band)
    value = dot(jnp.concatenate([high, low, high], axis=1), right_t)
    high, low = split(value)
    return dot(left_t, jnp.concatenate([high, low, high], axis=0))


def momentum_kernel(moment_ref, c_ref, left_ref, right_ref, out_ref):
    for j in range(N_WIDE):
        columns, bands = slice(j * WIDE, (j + 1) * WIDE), slice(j * NARROW, (j + 1) * NARROW)
        out_ref[0, :, columns] = moment_ref[:, columns] - field_of(
            c_ref[:, bands], left_ref[...], right_ref[...]
        )


def momentum_less_band(moment, coeffs, table, **order):
    return call(
        momentum_kernel,
        [
            (moment, VMEM),
            (coeffs, VMEM),
            (table["left_t"], VMEM),
            (table["right_t"], VMEM),
        ],
        [((1, ROWS, COLS), f32, VMEM)],
        name="momentum_less_band",
        held=[(1, ROWS, COLS)],
        **order,
    )


def update_kernel(mine_ref, theirs_ref, left_ref, right_ref, out_ref):
    is_first = core_of() == 0
    mine, theirs = mine_ref[...] / N_REP, theirs_ref[...] / N_REP
    first = jnp.where(is_first, mine, theirs)
    second = jnp.where(is_first, theirs, mine)
    full = jnp.concatenate([first, second], axis=1)
    for j in range(N_WIDE):
        columns, bands = slice(j * WIDE, (j + 1) * WIDE), slice(j * NARROW, (j + 1) * NARROW)
        out_ref[:, columns] = field_of(full[:, bands], left_ref[...], right_ref[...])


def update_of(mine, theirs, table, **order):
    return call(
        update_kernel,
        [(mine, VMEM), (theirs, VMEM), (table["left_t"], VMEM), (table["right_t"], VMEM)],
        [((ROWS, COLS), f32, VMEM)],
        name="update",
        held=[(ROWS, COLS)],
        **order,
    )


SIDES = (3, 0, 1, 2)


def input_band_kernel(x_ref, pair_ref, high_ref, low_ref, turned_ref, held, pair, sems):
    def copy(j):
        columns = pl.ds(j * WIDE, WIDE)
        return pltpu.make_async_copy(x_ref.at[0, :, columns], held.at[:, columns], sems.at[j])

    table = pltpu.make_async_copy(pair_ref, pair, sems.at[N_WIDE])
    table.start()
    for j in range(N_WIDE):
        copy(j).start()
    table.wait()
    for j in range(N_WIDE):
        copy(j).wait()
        both = dot(held[:, j * WIDE : (j + 1) * WIDE], pair[...])
        bands = slice(j * NARROW, (j + 1) * NARROW)
        high_ref[:, bands], low_ref[:, bands] = split(both[:, :NARROW] + both[:, NARROW:])
    shard = lax.axis_index("fsdp")
    here, z = shard // 4, lax.rem(shard, 4)
    wide = COLS // 2
    for k in range(4):

        @pl.when(z == k)
        def _():
            for part, x in enumerate((here, 1 - here)):
                source = held[:, pl.ds(pl.multiple_of(x * wide, NARROW), wide)]
                starts = [(k + side) % 4 * ROWS for side in SIDES]
                turned_ref[:, part * wide : (part + 1) * wide] = jnp.concatenate(
                    [source[:, start : start + ROWS] for start in starts], axis=1
                )


def input_band(inputs, table, **order):
    part = ((TOKENS, BANDS), bf16, VMEM)
    return call(
        input_band_kernel,
        [(inputs, ANY), (table["right_pair"], ANY)],
        [part, part, ((TOKENS, COLS), bf16, VMEM)],
        scratch=[
            pltpu.VMEM((TOKENS, COLS), bf16),
            pltpu.VMEM((WIDE, 2 * NARROW), bf16),
            pltpu.SemaphoreType.DMA((N_WIDE + 1,)),
        ],
        name="input_band",
        **order,
    )


def sum_kernel(*refs):
    total = refs[0][...]
    for ref in refs[1:-1]:
        total += ref[...]
    refs[-1][...] = total


def sum_of(parts, name, **order):
    return call(
        sum_kernel,
        [(part, VMEM) for part in parts],
        [(parts[0].shape, f32, VMEM)],
        name=name,
        **order,
    )


def pair_kernel(own_ref, opposite_ref, left_ref, right_ref, own_out, pair_ref):
    own = own_ref[...] + opposite_ref[...]
    other = left_ref[...] + right_ref[...]
    own_out[...] = own
    is_first = lax.axis_index("fsdp") < 4
    pair_ref[:TILE_ROWS] = jnp.where(is_first, own, other).astype(bf16)
    pair_ref[TILE_ROWS:] = jnp.where(is_first, other, own).astype(bf16)


def pair_of(own, opposite, left, right, **order):
    return call(
        pair_kernel,
        [(part, VMEM) for part in (own, opposite, left, right)],
        [((TILE_ROWS, HALF), f32, VMEM), ((2 * TILE_ROWS, HALF), bf16, VMEM)],
        name="pair",
        **order,
    )


def pack_kernel(*refs):
    row = 0
    for ref in refs[:-1]:
        refs[-1][row : row + ref.shape[0]] = ref[...]
        row += ref.shape[0]


def pack(arrays, name, **order):
    shape = (sum(array.shape[0] for array in arrays), arrays[0].shape[1])
    return call(
        pack_kernel,
        [(array, VMEM) for array in arrays],
        [(shape, arrays[0].dtype, VMEM)],
        name=name,
        **order,
    )


def hand_on_kernel():
    pass


def hand_on(arrays, after, name):
    return call(hand_on_kernel, [], [], name=name, after=after, through=arrays)[1:]


def change_kernel(high_ref, low_ref, bands_ref, s_bands_ref, out_ref, total):
    core = core_of()
    z = lax.rem(lax.axis_index("fsdp"), 4)
    for k, side in enumerate((0, 3, 1, 2)):
        source = lax.rem(z + side, 4)
        for x in range(2):
            row = pl.multiple_of((x * 4 + source) * TILE_ROWS, 16)
            rows = slice((2 * k + x) * TILE_ROWS, (2 * k + x + 1) * TILE_ROWS)
            total[core, pl.ds(row, TILE_ROWS)] = bands_ref[rows]
            total[1 - core, pl.ds(row, TILE_ROWS)] = s_bands_ref[rows]
    for half in range(2):
        value = dot(high_ref[...], total[half]) + dot(low_ref[...], total[half])
        for k in range(5):
            high, low = split(value[:, k * 64 : (k + 1) * 64])
            start = (half * 5 + k) * 256
            out_ref[:, start : start + 256] = jnp.concatenate([high, low, high, low], axis=1)


def change_of(high, low, bands, s_bands, **order):
    return call(
        change_kernel,
        [(array, VMEM) for array in (high, low, bands, s_bands)],
        [((TOKENS, COLS), bf16, VMEM)],
        scratch=[pltpu.VMEM((2, BANDS, HALF), bf16)],
        name="change",
        **order,
    )


BLOCK = 512
N_BLOCKS = COLS // BLOCK


def beside(core, first, s_first, second, s_second, columns):
    is_first = core == 0
    a, sa, b, sb = (ref[:, columns] for ref in (first, s_first, second, s_second))
    before = [jnp.where(is_first, a, sa), jnp.where(is_first, b, sb)]
    behind = [jnp.where(is_first, sb, b), jnp.where(is_first, sa, a)]
    return before, behind


def in_order(core, one, other, columns):
    is_first = core == 0
    a, b = one[:, columns], other[:, columns]
    return [jnp.where(is_first, a, b), jnp.where(is_first, b, a)]


def part_of(ref, start, rows=HALF_ROWS):
    return ref.at[pl.ds(start, rows)]


def own_kernel(x_ref, w_ref, z0, sz0, z1, z2, s_pack, held_ref, out_ref, final_ref, sem):
    core = core_of()
    flush = pltpu.make_async_copy(held_ref, final_ref, sem)
    flush.start()
    sz1, sz2 = part_of(s_pack, 0), part_of(s_pack, HALF_ROWS)
    for n in range(N_BLOCKS):
        columns = slice(n * BLOCK, (n + 1) * BLOCK)
        before, behind = beside(core, z0, sz0, z1, sz1, columns)
        rows = before + [w_ref[:, columns]] + behind + in_order(core, z2, sz2, columns)
        out_ref[:, columns] = dot(x_ref[:, : 4 * ROWS], jnp.concatenate(rows, axis=0))
    flush.wait()


def own_product(turned, pieces, held, **order):
    return call(
        own_kernel,
        [(array, VMEM) for array in (turned, *pieces, held)],
        [((TOKENS, COLS), f32, VMEM), (held.shape, f32, ANY)],
        scratch=[pltpu.SemaphoreType.DMA],
        name="own_product",
        **order,
    )


def near_kernel(x_ref, acc_ref, change_ref, step_ref, x0, z0, z1, s_pack, sz1, out_ref):
    core = core_of()
    sz0, sx0 = part_of(s_pack, 2 * HALF_ROWS), part_of(s_pack, 3 * HALF_ROWS)
    for n in range(N_BLOCKS):
        columns = slice(n * BLOCK, (n + 1) * BLOCK)
        before, behind = beside(core, z0, sz0, z1, sz1, columns)
        rows = before + in_order(core, x0, sx0, columns) + behind
        value = dot(x_ref[:, 4 * ROWS : 7 * ROWS], jnp.concatenate(rows, axis=0))
        change = change_ref[:, columns]
        steps = [dot(change[:, k : k + 256], step_ref[...]) for k in (0, 256)]
        out_ref[:, columns] = acc_ref[:, columns] + value + jnp.concatenate(steps, axis=1)


def near_product(turned, acc, change, pieces, table, **order):
    return call(
        near_kernel,
        [(array, VMEM) for array in (turned, acc, change, table["step"], *pieces)],
        [((TOKENS, COLS), f32, VMEM)],
        name="near_product",
        **order,
    )


def far_kernel(
    x_ref, acc_ref, top, low, s_last, held_ref,
    out_ref, final_ref, result, sems,
):
    core = core_of()
    s_top, s_low = part_of(s_last, 0, QUARTER), part_of(s_last, QUARTER, QUARTER)
    flush = pltpu.make_async_copy(held_ref, final_ref, sems.at[N_BLOCKS])
    flush.start()

    def write(n):
        columns = pl.ds(n * BLOCK, BLOCK)
        return pltpu.make_async_copy(
            result.at[:, columns], out_ref.at[0, :, columns], sems.at[n]
        )

    for n in range(N_BLOCKS):
        columns = slice(n * BLOCK, (n + 1) * BLOCK)
        tops, lows = in_order(core, top, s_top, columns), in_order(core, low, s_low, columns)
        rows = jnp.concatenate([tops[0], lows[0], tops[1], lows[1]], axis=0)
        value = dot(x_ref[:, 7 * ROWS :], rows)
        result[:, columns] = (acc_ref[:, columns] + value).astype(bf16)
        write(n).start()
    for n in range(N_BLOCKS):
        write(n).wait()
    flush.wait()


def far_product(turned, acc, pieces, held, **order):
    return call(
        far_kernel,
        [(array, VMEM) for array in (turned, acc, *pieces, held)],
        [((1, TOKENS, COLS), bf16, ANY), (held.shape, f32, ANY)],
        scratch=[pltpu.VMEM((TOKENS, COLS), bf16), pltpu.SemaphoreType.DMA((N_BLOCKS + 1,))],
        name="far_product",
        **order,
    )


def swapped(value, axis, step):
    pairs = []
    for device in range(128):
        place = list(place_of(device))
        place[axis] = 3 - place[axis] if step else place[axis] ^ 1
        pairs.append((device, device_at(*place)))
    return lax.ppermute(value, BOTH, pairs)


def shards(momentum, gradient, weights, inputs):
    table = {
        name: pltpu.with_memory_space_constraint(jnp.asarray(value), pltpu.HBM)
        if name in ("left", "right", "right_pair")
        else value
        for name, value in tables().items()
    }
    momentum, gradient, weights, inputs = (
        pltpu.with_memory_space_constraint(array, pltpu.HBM)
        for array in (momentum, gradient, weights, inputs)
    )

    coeffs, mine, theirs, moment, first, second, _ = band(momentum, gradient, weights, table)
    z0 = along_z(first)
    x0 = along_x(first)
    z1 = along_z(second)
    chip, _ = sum_of([mine, across(theirs)], "chip_sum")
    half_y = swapped(chip, 1, 0)
    high, low, turned, done = input_band(inputs, table, after=[chip])
    half_sum, _, z0, x0 = sum_of(
        [chip, half_y], "half_y_sum", after=[done], through=[z0, x0]
    )
    rest_y = swapped(half_sum, 1, 1)
    xz0 = along_x(z0)
    z2 = along_z(z0)
    sz0 = across(z0)
    column, _, z1, sz0 = sum_of([half_sum, rest_y], "y_sum", through=[z1, sz0])
    x_parts = by(column, 0, 2), by(column, 0, 1), by(column, 0, -1)
    new_momentum, done = momentum_less_band(moment, coeffs, table, after=[column])
    own, pair, _, xz0, z2 = pair_of(column, *x_parts, after=[done], through=[xz0, z2])
    z_parts = by(pair, 2, 1), by(pair, 2, -1), by(pair, 2, 2)
    xz1 = along_x(z1)
    near, done = pack([z1, z2, xz0, x0], "pack_near", after=[pair])
    s_near = across(near)
    acc, new_momentum, done = own_product(
        turned, [weights, z0, sz0, z1, z2, s_near], new_momentum, after=[done]
    )
    bands, done = pack([pair, *z_parts], "pack_bands", after=[done])
    s_bands = across(bands)
    xz2 = along_x(z2[:QUARTER])
    z3 = along_z(xz0[QUARTER:])
    xz1, own = hand_on([xz1, own], [done], "after_pack_bands")
    sxz1, s_own = across(xz1), across(own)
    change, done = change_of(high, low, bands, s_bands, after=[own])
    acc, done, s_own = near_product(
        turned, acc, change, [x0, xz0, xz1, s_near, sxz1], table, after=[done], through=[s_own]
    )
    last, done = pack([xz2, z3], "pack_last", after=[done])
    s_last = across(last)
    update, done = update_of(own, s_own, table, after=[done])
    result, update, _ = far_product(turned, acc, [xz2, z3, s_last], update, after=[done])
    return (new_momentum, update, result)


def solution(mesh):
    placed = (
        P("rep", "fsdp", None),
        P("rep", "fsdp", None),
        P("fsdp", None),
        P("rep", "fsdp", None),
    )
    return jax.shard_map(
        shards,
        mesh=mesh,
        in_specs=placed,
        out_specs=(P("rep", "fsdp", None), P("fsdp", None), P("rep", "fsdp", None)),
        check_vma=False,
    )
```

```python
import functools
import math

import jax
import jax.numpy as jnp
import ml_dtypes
import numpy as np
from jax import lax
from jax.experimental import pallas as pl
from jax.experimental.pallas import tpu as pltpu
from jax.sharding import PartitionSpec as P

f32, bf16 = jnp.float32, jnp.bfloat16
BOTH = ("rep", "fsdp")
decay = 0.9
step_size = 0.1
ROWS, COLS, TOKENS = 320, 2560, 640
BANDS = 16 * COLS // 64
TILE_ROWS = 16 * ROWS // 64
HALF = BANDS // 2
WIDE = 512
NARROW = 128
N_REP = 16


def place_of(device):
    rep, shard = divmod(device, 8)
    return (rep // 2 % 2) * 2 + shard // 4, rep // 4, shard % 4, rep % 2


def device_at(x, y, z, core):
    x, y, z = x % 4, y % 4, z % 4
    return ((y * 2 + x // 2) * 2 + core % 2) * 8 + (x % 2) * 4 + z


def moved(value, first, second=None):
    pairs = []
    for device in range(128):
        x, y, z, core = place_of(device)
        dx, dy, dz, dc = first if second is None or core == 0 else second
        pairs.append((device, device_at(x + dx, y + dy, z + dz, core + dc)))
    return lax.ppermute(value, BOTH, pairs)


def along_z(value):
    return moved(value, (0, 0, 1, 0), (0, 0, -1, 0))


def along_x(value):
    return moved(value, (1, 0, 0, 0), (-1, 0, 0, 0))


def across(value):
    return moved(value, (0, 0, 0, 1))


def by(value, axis, distance):
    return moved(value, tuple(distance if k == axis else 0 for k in range(4)))


def basis_table():
    freq = np.arange(16)[:, None]
    spot = np.arange(64)[None, :]
    table = np.cos(math.pi * (2 * spot + 1) * freq / 128) * math.sqrt(2 / 64)
    table[0] = math.sqrt(1 / 64)
    return table


def halves(table):
    high = table.astype(ml_dtypes.bfloat16)
    low = (table - high.astype(np.float64)).astype(ml_dtypes.bfloat16)
    return high, low


def tables():
    basis = basis_table()
    left_high, left_low = halves(np.kron(np.eye(ROWS // 64), basis))
    right_high, right_low = halves(np.kron(np.eye(WIDE // 64), basis.T))
    step_high, step_low = halves(np.kron(np.eye(4), basis) * (-step_size / N_REP))
    return {
        "left": np.concatenate([left_high, left_low], 0),
        "right": np.stack([right_high, right_low]),
        "left_t": np.concatenate([left_high.T, left_high.T, left_low.T], 1),
        "right_t": np.concatenate([right_high.T, right_high.T, right_low.T], 0),
        "right_pair": np.concatenate([right_high, right_low], 1),
        "step": np.concatenate([step_high, step_high, step_low, step_low], 0),
    }


def dot(a, b):
    return jnp.dot(a, b, preferred_element_type=f32)


def split(value):
    high = value.astype(bf16)
    return high, (value - high.astype(f32)).astype(bf16)


def core_of():
    return lax.rem(lax.axis_index("rep"), 2)


def whole(shape):
    return pl.BlockSpec(shape, lambda j: (0,) * len(shape))


ANY = pl.BlockSpec(memory_space=pl.ANY)
VMEM = pl.BlockSpec(memory_space=pltpu.VMEM)


def params(megabytes):
    return pltpu.CompilerParams(vmem_limit_bytes=megabytes * 2**20)


def call(kernel, ins, outs, scratch=(), grid=(), megabytes=24, name=None, after=(), through=(), cost=1, held=()):
    n_in, n_out, n_extra = len(ins), len(outs), len(after) + len(through)
    token = ((8, 128), f32, whole((8, 128)) if grid else VMEM)

    def body(*refs):
        n = n_in + n_extra
        token_ref = refs[n + n_out]
        token_ref[...] = jnp.zeros(token_ref.shape, f32)
        kernel(*refs[:n_in], *refs[n : n + n_out], *refs[n + n_out + 1 + len(through) :])

    return pl.pallas_call(
        body,
        grid=grid,
        out_shape=tuple(
            pltpu.VMEM(shape, dtype) if spec is VMEM and shape in held else jax.ShapeDtypeStruct(shape, dtype)
            for shape, dtype, spec in (*outs, token)
        )
        + tuple(jax.ShapeDtypeStruct(array.shape, array.dtype) for array in through),
        in_specs=[spec for _, spec in ins] + [ANY] * n_extra,
        out_specs=tuple(spec for _, _, spec in (*outs, token)) + (ANY,) * len(through),
        scratch_shapes=list(scratch),
        input_output_aliases={
            n_in + len(after) + k: n_out + 1 + k for k in range(len(through))
        },
        compiler_params=params(megabytes),
        cost_estimate=pl.CostEstimate(flops=cost, transcendentals=0, bytes_accessed=1),
        name=name,
    )(*[array for array, _ in ins], *after, *through)


def column_block(rows, width):
    return pl.BlockSpec((rows, width), lambda j: (0, j))


def column_block_of_one(rows, width):
    return pl.BlockSpec((1, rows, width), lambda j: (0, 0, j))


N_WIDE = COLS // WIDE
HALF_ROWS = ROWS // 2
QUARTER = ROWS // 4


def band_kernel(
    m_ref, g_ref, w_ref, left_ref, right_ref,
    c_ref, mine_ref, theirs_ref, moment_ref, first_ref, second_ref,
    g_buffer, left, right, sems,
):
    core = core_of()

    def copies(j):
        columns = pl.ds(j * WIDE, WIDE)
        return (
            pltpu.make_async_copy(m_ref.at[0, :, columns], moment_ref.at[:, columns], sems.at[2 * j]),
            pltpu.make_async_copy(g_ref.at[0, :, columns], g_buffer.at[:, columns], sems.at[2 * j + 1]),
        )

    def rows(which):
        return w_ref.at[pl.ds(pl.multiple_of(which * HALF_ROWS, HALF_ROWS), HALF_ROWS)]

    base = 2 * N_WIDE
    others = (
        pltpu.make_async_copy(left_ref, left, sems.at[base]),
        pltpu.make_async_copy(right_ref, right, sems.at[base + 1]),
        pltpu.make_async_copy(rows(core), first_ref, sems.at[base + 2]),
        pltpu.make_async_copy(rows(1 - core), second_ref, sems.at[base + 3]),
    )
    for copy in (*others[:2], *copies(0), *copies(1), *copies(2), *copies(3), *copies(4), *others[2:]):
        copy.start()
    for copy in others[:2]:
        copy.wait()
    for j in range(N_WIDE):
        for copy in copies(j):
            copy.wait()
        columns = slice(j * WIDE, (j + 1) * WIDE)
        moment = decay * moment_ref[:, columns] + g_buffer[:, columns].astype(f32)
        moment_ref[:, columns] = moment
        high, low = split(moment)
        both = dot(left[...], high)
        value = both[:TILE_ROWS] + both[TILE_ROWS:] + dot(left[:TILE_ROWS], low)
        high, low = split(value)
        c_ref[:, j * NARROW : (j + 1) * NARROW] = (
            dot(high, right[0]) + dot(high, right[1]) + dot(low, right[0])
        )
    is_first = core == 0
    one, two = c_ref[:, :HALF], c_ref[:, HALF:]
    mine_ref[...] = jnp.where(is_first, one, two)
    theirs_ref[...] = jnp.where(is_first, two, one)
    for copy in others[2:]:
        copy.wait()


def band(momentum, gradient, weights, table, **order):
    part = ((TILE_ROWS, HALF), f32, VMEM)
    rows = ((HALF_ROWS, COLS), bf16, VMEM)
    return call(
        band_kernel,
        [(array, ANY) for array in (momentum, gradient, weights, table["left"], table["right"])],
        [((TILE_ROWS, BANDS), f32, VMEM), part, part, ((ROWS, COLS), f32, VMEM), rows, rows],
        scratch=[
            pltpu.VMEM((ROWS, COLS), bf16),
            pltpu.VMEM((2 * TILE_ROWS, ROWS), bf16),
            pltpu.VMEM((2, WIDE, NARROW), bf16),
            pltpu.SemaphoreType.DMA((2 * N_WIDE + 4,)),
        ],
        name="band",
        **order,
    )


def field_of(band, left_t, right_t):
    high, low = split(band)
    value = dot(jnp.concatenate([high, low, high], axis=1), right_t)
    high, low = split(value)
    return dot(left_t, jnp.concatenate([high, low, high], axis=0))


def momentum_kernel(moment_ref, c_ref, left_ref, right_ref, out_ref):
    for j in range(N_WIDE):
        columns, bands = slice(j * WIDE, (j + 1) * WIDE), slice(j * NARROW, (j + 1) * NARROW)
        out_ref[0, :, columns] = moment_ref[:, columns] - field_of(
            c_ref[:, bands], left_ref[...], right_ref[...]
        )


def momentum_less_band(moment, coeffs, table, **order):
    return call(
        momentum_kernel,
        [
            (moment, VMEM),
            (coeffs, VMEM),
            (table["left_t"], VMEM),
            (table["right_t"], VMEM),
        ],
        [((1, ROWS, COLS), f32, VMEM)],
        name="momentum_less_band",
        held=[(1, ROWS, COLS)],
        **order,
    )


def update_kernel(mine_ref, theirs_ref, left_ref, right_ref, out_ref):
    is_first = core_of() == 0
    start = pl.multiple_of(lax.axis_index("fsdp") // 4 * TILE_ROWS, 16)
    rows = pl.ds(start, TILE_ROWS)
    mine, theirs = (ref[rows].astype(f32) / N_REP for ref in (mine_ref, theirs_ref))
    first = jnp.where(is_first, mine, theirs)
    second = jnp.where(is_first, theirs, mine)
    full = jnp.concatenate([first, second], axis=1)
    for j in range(N_WIDE):
        columns, bands = slice(j * WIDE, (j + 1) * WIDE), slice(j * NARROW, (j + 1) * NARROW)
        out_ref[:, columns] = field_of(full[:, bands], left_ref[...], right_ref[...])


def update_of(mine, theirs, table, **order):
    return call(
        update_kernel,
        [(mine, VMEM), (theirs, VMEM), (table["left_t"], VMEM), (table["right_t"], VMEM)],
        [((ROWS, COLS), f32, VMEM)],
        name="update",
        held=[(ROWS, COLS)],
        **order,
    )


SIDES = (3, 0, 1, 2)


def input_band_kernel(x_ref, pair_ref, band_ref, turned_ref, held, pair, sems):
    def copy(j):
        columns = pl.ds(j * WIDE, WIDE)
        return pltpu.make_async_copy(x_ref.at[0, :, columns], held.at[:, columns], sems.at[j])

    table = pltpu.make_async_copy(pair_ref, pair, sems.at[N_WIDE])
    table.start()
    for j in range(N_WIDE):
        copy(j).start()
    table.wait()
    for j in range(N_WIDE):
        copy(j).wait()
        both = dot(held[:, j * WIDE : (j + 1) * WIDE], pair[...])
        bands = slice(j * NARROW, (j + 1) * NARROW)
        band_ref[:, bands] = (both[:, :NARROW] + both[:, NARROW:]).astype(bf16)
    shard = lax.axis_index("fsdp")
    here, z = shard // 4, lax.rem(shard, 4)
    wide = COLS // 2
    for k in range(4):

        @pl.when(z == k)
        def _():
            for part, x in enumerate((here, 1 - here)):
                source = held[:, pl.ds(pl.multiple_of(x * wide, NARROW), wide)]
                starts = [(k + side) % 4 * ROWS for side in SIDES]
                turned_ref[:, part * wide : (part + 1) * wide] = jnp.concatenate(
                    [source[:, start : start + ROWS] for start in starts], axis=1
                )


def input_band(inputs, table, **order):
    part = ((TOKENS, BANDS), bf16, VMEM)
    return call(
        input_band_kernel,
        [(inputs, ANY), (table["right_pair"], ANY)],
        [part, ((TOKENS, COLS), bf16, VMEM)],
        scratch=[
            pltpu.VMEM((TOKENS, COLS), bf16),
            pltpu.VMEM((WIDE, 2 * NARROW), bf16),
            pltpu.SemaphoreType.DMA((N_WIDE + 1,)),
        ],
        name="input_band",
        **order,
    )


def sum_kernel(*refs):
    total = refs[0][...]
    for ref in refs[1:-1]:
        total += ref[...]
    refs[-1][...] = total


def sum_of(parts, name, **order):
    return call(
        sum_kernel,
        [(part, VMEM) for part in parts],
        [(parts[0].shape, f32, VMEM)],
        name=name,
        **order,
    )


def pair_kernel(own_ref, opposite_ref, left_ref, right_ref, pair_ref):
    own = own_ref[...] + opposite_ref[...]
    other = left_ref[...] + right_ref[...]
    is_first = lax.axis_index("fsdp") < 4
    pair_ref[:TILE_ROWS] = jnp.where(is_first, own, other).astype(bf16)
    pair_ref[TILE_ROWS:] = jnp.where(is_first, other, own).astype(bf16)


def pair_of(own, opposite, left, right, **order):
    return call(
        pair_kernel,
        [(part, VMEM) for part in (own, opposite, left, right)],
        [((2 * TILE_ROWS, HALF), bf16, VMEM)],
        name="pair",
        **order,
    )


def pack_kernel(*refs):
    row = 0
    for ref in refs[:-1]:
        refs[-1][row : row + ref.shape[0]] = ref[...]
        row += ref.shape[0]


def pack(arrays, name, **order):
    shape = (sum(array.shape[0] for array in arrays), arrays[0].shape[1])
    return call(
        pack_kernel,
        [(array, VMEM) for array in arrays],
        [(shape, arrays[0].dtype, VMEM)],
        name=name,
        **order,
    )


def hand_on_kernel():
    pass


def hand_on(arrays, after, name):
    return call(hand_on_kernel, [], [], name=name, after=after, through=arrays)[1:]


def change_kernel(high_ref, bands_ref, s_bands_ref, out_ref, total):
    core = core_of()
    z = lax.rem(lax.axis_index("fsdp"), 4)
    for k, side in enumerate((0, 3, 1, 2)):
        source = lax.rem(z + side, 4)
        for x in range(2):
            row = pl.multiple_of((x * 4 + source) * TILE_ROWS, 16)
            rows = slice((2 * k + x) * TILE_ROWS, (2 * k + x + 1) * TILE_ROWS)
            total[core, pl.ds(row, TILE_ROWS)] = bands_ref[rows]
            total[1 - core, pl.ds(row, TILE_ROWS)] = s_bands_ref[rows]
    for half in range(2):
        value = dot(high_ref[...], total[half])
        for k in range(5):
            high, low = split(value[:, k * 64 : (k + 1) * 64])
            start = (half * 5 + k) * 256
            out_ref[:, start : start + 256] = jnp.concatenate([high, low, high, low], axis=1)


def change_of(high, bands, s_bands, **order):
    return call(
        change_kernel,
        [(array, VMEM) for array in (high, bands, s_bands)],
        [((TOKENS, COLS), bf16, VMEM)],
        scratch=[pltpu.VMEM((2, BANDS, HALF), bf16)],
        name="change",
        **order,
    )


BLOCK = 512
N_BLOCKS = COLS // BLOCK


def beside(core, first, s_first, second, s_second, columns):
    is_first = core == 0
    a, sa, b, sb = (ref[:, columns] for ref in (first, s_first, second, s_second))
    before = [jnp.where(is_first, a, sa), jnp.where(is_first, b, sb)]
    behind = [jnp.where(is_first, sb, b), jnp.where(is_first, sa, a)]
    return before, behind


def in_order(core, one, other, columns):
    is_first = core == 0
    a, b = one[:, columns], other[:, columns]
    return [jnp.where(is_first, a, b), jnp.where(is_first, b, a)]


def part_of(ref, start, rows=HALF_ROWS):
    return ref.at[pl.ds(start, rows)]


def own_kernel(x_ref, w_ref, z0, sz0, z1, z2, s_pack, held_ref, out_ref, final_ref, sem):
    core = core_of()
    flush = pltpu.make_async_copy(held_ref, final_ref, sem)
    flush.start()
    sz1, sz2 = part_of(s_pack, 0), part_of(s_pack, HALF_ROWS)
    for n in range(N_BLOCKS):
        columns = slice(n * BLOCK, (n + 1) * BLOCK)
        before, behind = beside(core, z0, sz0, z1, sz1, columns)
        rows = before + [w_ref[:, columns]] + behind + in_order(core, z2, sz2, columns)
        out_ref[:, columns] = dot(x_ref[:, : 4 * ROWS], jnp.concatenate(rows, axis=0))
    flush.wait()


def own_product(turned, pieces, held, **order):
    return call(
        own_kernel,
        [(array, VMEM) for array in (turned, *pieces, held)],
        [((TOKENS, COLS), f32, VMEM), (held.shape, f32, ANY)],
        scratch=[pltpu.SemaphoreType.DMA],
        name="own_product",
        **order,
    )


def near_kernel(x_ref, acc_ref, change_ref, step_ref, x0, z0, z1, s_pack, sz1, out_ref):
    core = core_of()
    sz0, sx0 = part_of(s_pack, 2 * HALF_ROWS), part_of(s_pack, 3 * HALF_ROWS)
    for n in range(N_BLOCKS):
        columns = slice(n * BLOCK, (n + 1) * BLOCK)
        before, behind = beside(core, z0, sz0, z1, sz1, columns)
        rows = before + in_order(core, x0, sx0, columns) + behind
        value = dot(x_ref[:, 4 * ROWS : 7 * ROWS], jnp.concatenate(rows, axis=0))
        change = change_ref[:, columns]
        steps = [dot(change[:, k : k + 256], step_ref[...]) for k in (0, 256)]
        out_ref[:, columns] = acc_ref[:, columns] + value + jnp.concatenate(steps, axis=1)


def near_product(turned, acc, change, pieces, table, **order):
    return call(
        near_kernel,
        [(array, VMEM) for array in (turned, acc, change, table["step"], *pieces)],
        [((TOKENS, COLS), f32, VMEM)],
        name="near_product",
        **order,
    )


def far_kernel(
    x_ref, acc_ref, top, low, s_last, held_ref,
    out_ref, final_ref, result, sems,
):
    core = core_of()
    s_top, s_low = part_of(s_last, 0, QUARTER), part_of(s_last, QUARTER, QUARTER)
    flush = pltpu.make_async_copy(held_ref, final_ref, sems.at[N_BLOCKS])
    flush.start()

    def write(n):
        columns = pl.ds(n * BLOCK, BLOCK)
        return pltpu.make_async_copy(
            result.at[:, columns], out_ref.at[0, :, columns], sems.at[n]
        )

    for n in range(N_BLOCKS):
        columns = slice(n * BLOCK, (n + 1) * BLOCK)
        tops, lows = in_order(core, top, s_top, columns), in_order(core, low, s_low, columns)
        rows = jnp.concatenate([tops[0], lows[0], tops[1], lows[1]], axis=0)
        value = dot(x_ref[:, 7 * ROWS :], rows)
        result[:, columns] = (acc_ref[:, columns] + value).astype(bf16)
        write(n).start()
    for n in range(N_BLOCKS):
        write(n).wait()
    flush.wait()


def far_product(turned, acc, pieces, held, **order):
    return call(
        far_kernel,
        [(array, VMEM) for array in (turned, acc, *pieces, held)],
        [((1, TOKENS, COLS), bf16, ANY), (held.shape, f32, ANY)],
        scratch=[pltpu.VMEM((TOKENS, COLS), bf16), pltpu.SemaphoreType.DMA((N_BLOCKS + 1,))],
        name="far_product",
        **order,
    )


def swapped(value, axis, step):
    pairs = []
    for device in range(128):
        place = list(place_of(device))
        place[axis] = 3 - place[axis] if step else place[axis] ^ 1
        pairs.append((device, device_at(*place)))
    return lax.ppermute(value, BOTH, pairs)


def shards(momentum, gradient, weights, inputs):
    table = {
        name: pltpu.with_memory_space_constraint(jnp.asarray(value), pltpu.HBM)
        if name in ("left", "right", "right_pair")
        else value
        for name, value in tables().items()
    }
    momentum, gradient, weights, inputs = (
        pltpu.with_memory_space_constraint(array, pltpu.HBM)
        for array in (momentum, gradient, weights, inputs)
    )

    coeffs, mine, theirs, moment, first, second, _ = band(momentum, gradient, weights, table)
    z0 = along_z(first)
    x0 = along_x(first)
    z1 = along_z(second)
    chip, _ = sum_of([mine, across(theirs)], "chip_sum")
    half_y = swapped(chip, 1, 0)
    high, turned, done = input_band(inputs, table, after=[chip])
    half_sum, _, z0, x0 = sum_of(
        [chip, half_y], "half_y_sum", after=[done], through=[z0, x0]
    )
    rest_y = swapped(half_sum, 1, 1)
    xz0 = along_x(z0)
    z2 = along_z(z0)
    sz0 = across(z0)
    column, _, z1, sz0 = sum_of([half_sum, rest_y], "y_sum", through=[z1, sz0])
    x_parts = by(column, 0, 2), by(column, 0, 1), by(column, 0, -1)
    new_momentum, done = momentum_less_band(moment, coeffs, table, after=[column])
    pair, _, xz0, z2 = pair_of(column, *x_parts, after=[done], through=[xz0, z2])
    z_parts = by(pair, 2, 1), by(pair, 2, -1), by(pair, 2, 2)
    xz1 = along_x(z1)
    near, done = pack([z1, z2, xz0, x0], "pack_near", after=[pair])
    s_near = across(near)
    acc, new_momentum, done = own_product(
        turned, [weights, z0, sz0, z1, z2, s_near], new_momentum, after=[done]
    )
    bands, done = pack([pair, *z_parts], "pack_bands", after=[done])
    s_bands = across(bands)
    xz2 = along_x(z2[:QUARTER])
    z3 = along_z(xz0[QUARTER:])
    xz1, s_bands = hand_on([xz1, s_bands], [done], "after_pack_bands")
    sxz1 = across(xz1)
    change, done = change_of(high, bands, s_bands)
    acc, done = near_product(
        turned, acc, change, [x0, xz0, xz1, s_near, sxz1], table, after=[done]
    )
    last, done = pack([xz2, z3], "pack_last", after=[done])
    s_last = across(last)
    update, done = update_of(bands, s_bands, table, after=[done])
    result, update, _ = far_product(turned, acc, [xz2, z3, s_last], update, after=[done])
    return (new_momentum, update, result)


def solution(mesh):
    placed = (
        P("rep", "fsdp", None),
        P("rep", "fsdp", None),
        P("fsdp", None),
        P("rep", "fsdp", None),
    )
    return jax.shard_map(
        shards,
        mesh=mesh,
        in_specs=placed,
        out_specs=(P("rep", "fsdp", None), P("fsdp", None), P("rep", "fsdp", None)),
        check_vma=False,
    )
```
